256 devices in a mesh: dp: 16 (over x_lo, y, core), tensor: 16 (over z, x_hi).
Axes of the slice: x: 4 (x_hi: 2, x_lo: 2; x = x_hi * 2 + x_lo), y: 4, z: 8, core: 2. Of those that a mesh axis runs over, the one named last changes fastest.
Arguments:
- hidden: bfloat16 [32768, 14336], P('dp', 'tensor'), may hold values from -3 to 3
- final_states: bfloat16 [32768, 4096], P(('dp', 'tensor')), may hold values from -6 to 6
- logp_grad: bfloat16 [32768, 4096], P(('dp', 'tensor')), may hold values from -0.09375 to 0.09375
- value_weight: bfloat16 [4096], replicated, may hold values from -0.09375 to 0.09375
- returns: float32 [32768], P(('dp', 'tensor')), may hold values from -6 to 6
- advantages: float32 [32768], P(('dp', 'tensor')), may hold values from -6 to 10
- log_ratio: float32 [32768], P(('dp', 'tensor')), may hold values from -1 to 1
- lengths: int32 [16], replicated, may hold values from 1 to 2048, 24576 in all
Outputs:
- grad_down: bfloat16 [14336, 4096], P(('tensor', 'dp'))
The draws below stay inside these ranges and needn't reach their ends.
Inputs may be any that keep to these rules, and one draw needn't show every extreme that they name: `lengths`: each data group's response length; some group's response is exactly 2048 long.
All inputs are finite; a program needn't handle non-finite values.
Results may differ from the reference program's by a relative error of at most 0.022.
Values may be sent and summed in bfloat16 or wider, within the bound.
No kernel may reach another device: no remote copies, remote signals or barrier semaphores. Data moves between devices by JAX's collectives and lax.ppermute only.
A program may use at most 128 MiB of HBM per device.

```python
import math
import jax
import jax.numpy as jnp
import numpy as np
from jax import lax

D = 4096
FFW = 14336
TOK_GRP = 2048
TOKENS = 32768
N_DP = 16


def draw_advantages(key, part):
    key = jax.random.fold_in(key, 11)
    position = jnp.arange(TOKENS, dtype=jnp.float32) / TOKENS
    noise = jnp.clip(jax.random.normal(key, (TOKENS,), jnp.float32), -3.0, 3.0)
    spread_rate = 0.4 * jnp.exp(jnp.log(6.0) * position)
    centre = 0.5 + 1.5 * position
    return (centre + spread_rate * noise).astype(jnp.float32)


def levels(own_key, dims, split, low, top_value):
    factor_of, own = 1.0, jax.random.fold_in(own_key, 6)
    for axis_at, blocks in split:
        heights = jnp.exp(jax.random.uniform(jax.random.fold_in(own, axis_at), (blocks,), jnp.float32, low / len(split), top_value / len(split)))
        factor_of = factor_of * jnp.repeat(heights, dims[axis_at] // blocks).reshape([-1 if axis == axis_at else 1 for axis in range(len(dims))])
    return factor_of


def profile(number_of, total, limit, lean):
    weights = [(1 << 20) // math.isqrt(rank ** lean) + 1 for rank in range(2, number_of + 1)]
    surplus, counts = total - limit - (number_of - 1), [1] * (number_of - 1)
    while surplus > 0:
        candidates = [i for i in range(number_of - 1) if counts[i] < limit]
        pool, budget = sum([weights[i] for i in candidates]), surplus
        for i in candidates:
            extra = min(limit - counts[i], max(1, budget * weights[i] // pool), surplus)
            counts[i] = counts[i] + extra
            surplus = surplus - extra
    return np.array([limit] + counts)


def uneven(key, number_of, total, most, slope):
    if number_of == 2:
        one = jax.random.randint(key, (), max(1, total - most), min(most, total - 1) + 1)
        return jnp.stack([one, total - one])
    sizes = jnp.asarray(profile(number_of, total, most, slope), jnp.int32)
    pairs = (number_of - 1) // 2
    donor, taker = sizes[1:1 + 2 * pairs:2], sizes[2:2 + 2 * pairs:2]
    room = jnp.minimum(donor - 1, most - taker)
    moved = jax.random.randint(jax.random.fold_in(key, 1), (pairs,), 0, 1 << 20) % (room + 1)
    sizes = sizes.at[1:1 + 2 * pairs:2].set(donor - moved).at[2:2 + 2 * pairs:2].set(taker + moved)
    return sizes[jax.random.permutation(jax.random.fold_in(key, 2), number_of)]


def normal_values(key, dims, scale, bound, shards=(), kind=jnp.bfloat16):
    entries = jax.random.normal(key, dims, jnp.float32) * scale
    if len(shards) > 0:
        entries = levels(key, dims, shards, -0.22, 0.18) * entries
    return jnp.clip(entries, min=-bound, max=bound).astype(kind)


def setup_inputs(seed: int = 0) -> dict:
    streams_of = jax.random.split(jax.random.key(seed), 9)
    hidden = normal_values(streams_of[0], (TOKENS, FFW), 0.5, 3.0, ((0, 16), (1, 16)))
    final_states = normal_values(streams_of[1], (TOKENS, D), 1.0, 6.0, ((0, 256),))
    logp_grad = normal_values(streams_of[2], (TOKENS, D), D ** -0.5, 0.09375, ((0, 256),))
    value_weight = normal_values(streams_of[3], (D,), D ** -0.5, 0.09375)
    returns = normal_values(streams_of[4], (TOKENS,), 1.0, 6.0, ((0, 256),), jnp.float32)
    advantages = draw_advantages(jax.random.fold_in(streams_of[8], 71), 0)
    log_ratio = normal_values(streams_of[6], (TOKENS,), 0.2, 1.0, ((0, 256),), jnp.float32)
    lengths = uneven(streams_of[7], N_DP, N_DP * TOK_GRP * 3 // 4, TOK_GRP, 0).astype(jnp.int32)
    return {"hidden": hidden, "final_states": final_states, "logp_grad": logp_grad, "value_weight": value_weight, "returns": returns, "advantages": advantages, "log_ratio": log_ratio, "lengths": lengths}


def reference(hidden, final_states, logp_grad, value_weight, returns, advantages, log_ratio, lengths):
    indices = jnp.arange(TOKENS, dtype=jnp.int32)
    place = indices % TOK_GRP
    group = indices // TOK_GRP
    live_mask = (place < lengths[group]).astype(jnp.float32)
    values = jnp.dot(final_states, value_weight, preferred_element_type=jnp.float32)
    total_live = jnp.sum(live_mask)
    average = jnp.sum(live_mask * advantages) / total_live
    deviation = advantages - average
    spread = jnp.sum(live_mask * deviation * deviation) / total_live
    whitened = deviation * lax.rsqrt(spread + 1e-05)
    clipped = (whitened > 0) & (log_ratio > jnp.log(1.2)) | (whitened < 0) & (log_ratio < jnp.log(0.8))
    active = jnp.where(clipped, 0.0, 1.0).astype(jnp.float32)
    policy_scale = -live_mask * jnp.exp(log_ratio) * whitened * active
    value_scale = 0.5 * live_mask * (values - returns)
    grad_rows = (policy_scale[:, None] * logp_grad.astype(jnp.float32) + value_scale[:, None] * value_weight.astype(jnp.float32)[None, :]).astype(jnp.bfloat16)

    def add_group(total, group_index):
        first_row = (group_index * TOK_GRP).astype(jnp.int32)
        hidden_rows = lax.dynamic_slice_in_dim(hidden, first_row, TOK_GRP, 0)
        grad_part = lax.dynamic_slice_in_dim(grad_rows, first_row, TOK_GRP, 0)
        term = lax.dot_general(hidden_rows, grad_part, (((0,), (0,)), ((), ())), preferred_element_type=jnp.float32)
        rounded = lax.optimization_barrier(term.astype(jnp.bfloat16))
        return (total + rounded.astype(jnp.float32), None)
    total, _ = lax.scan(add_group, jnp.zeros((FFW, D), jnp.float32), jnp.arange(N_DP, dtype=jnp.int32))
    return total.astype(jnp.bfloat16)
```

```python
import jax
import jax.numpy as jnp
from jax import lax
from jax.sharding import Mesh, PartitionSpec as P

AXES = ("xl", "y", "c", "z", "xh")
CHUNKS = 4


def flip(v, axis):
    return lax.ppermute(v, axis, [(0, 1), (1, 0)])


def shift(v, axis, n, by):
    return lax.ppermute(v, axis, [(i, (i + by) % n) for i in range(n)])


def pair(v, axis, n, mask):
    return lax.ppermute(v, axis, [(i, i ^ mask) for i in range(n)])


def pick(v, index, axis):
    return lax.dynamic_index_in_dim(v, index, axis, keepdims=False)


def plus(a, b):
    return (a.astype(jnp.float32) + b.astype(jnp.float32)).astype(jnp.bfloat16)


def token_scales(final_states, value_weight, returns, advantages, log_ratio, lengths):
    rows = final_states.shape[0]
    xl, y, c, z, xh = (lax.axis_index(a) for a in AXES)
    group = (xl * 4 + y) * 2 + c
    start = (2 * z + xh) * rows
    live_here = (start + jnp.arange(rows, dtype=jnp.int32) < lengths[group]).astype(jnp.float32)
    values = jnp.dot(final_states, value_weight, preferred_element_type=jnp.float32)
    value_scale = 0.5 * live_here * (values - returns)
    own = jnp.stack([advantages, log_ratio, value_scale])
    both = jnp.stack([own, flip(own, "c")])
    column = jnp.stack([both] + [shift(both, "z", 8, j) for j in range(1, 8)])
    back = (z - jnp.arange(8, dtype=jnp.int32)) % 8
    column = jnp.take(column, back, axis=0)
    adv, ratio, vscale = column[:, :, 0], column[:, :, 1], column[:, :, 2]
    place = (
        (2 * jnp.arange(8, dtype=jnp.int32)[:, None, None] + xh) * rows
        + jnp.arange(rows, dtype=jnp.int32)[None, None, :]
    )
    limits = jnp.stack([lengths[group], lengths[group ^ 1]])[None, :, None]
    live = (place < limits).astype(jnp.float32)
    count = jnp.sum(live)
    total = jnp.sum(live * adv)
    mean = total / jnp.maximum(count, 1.0)
    centred = adv - mean
    moment = jnp.sum(live * centred * centred)
    part = jnp.stack([count, total, moment])
    part = jnp.stack([part] + [shift(part, "y", 4, j) for j in range(1, 4)])
    part = jnp.stack([part] + [shift(part, ("xl", "xh"), 4, j) for j in range(1, 4)]).reshape(16, 3)
    counts, totals, moments = part[:, 0], part[:, 1], part[:, 2]
    total_live = jnp.sum(counts)
    average = jnp.sum(totals) / total_live
    off = totals / jnp.maximum(counts, 1.0) - average
    spread = jnp.sum(moments + counts * off * off) / total_live
    whitened = (adv - average) * lax.rsqrt(spread + 1e-05)
    clipped = (whitened > 0) & (ratio > jnp.log(1.2)) | (whitened < 0) & (ratio < jnp.log(0.8))
    active = jnp.where(clipped, 0.0, 1.0).astype(jnp.float32)
    policy_scale = -live * jnp.exp(ratio) * whitened * active
    return policy_scale, vscale


def scatter_y(part, y, mask):
    other = mask ^ 2
    sent = jnp.stack([pick(part, y ^ mask, 1), pick(part, y ^ 2, 1)])
    got = pair(sent, "y", 4, mask)
    passed = plus(pick(part, y ^ other, 1), got[1])
    kept = plus(pick(part, y, 1), got[0])
    return plus(kept, pair(passed, "y", 4, other))


def scatter_x(quarter, xl):
    x = ("xl", "xh")
    w = quarter.shape[-1] // 2
    a, b = quarter[..., :w], quarter[..., w:]
    sent_a = jnp.stack([pick(a[0], 1 - xl, 0), pick(a[1], xl, 0)])
    sent_b = jnp.stack([pick(b[1], 1 - xl, 0), pick(b[1], xl, 0)])
    got_a = pair(sent_a, x, 4, 2)
    got_b = pair(sent_b, x, 4, 3)
    passed_a = plus(pick(a[1], 1 - xl, 0), got_a[1])
    passed_b = plus(pick(b[0], 1 - xl, 0), got_b[1])
    kept_a = plus(pick(a[0], xl, 0), got_a[0])
    kept_b = plus(pick(b[0], xl, 0), got_b[0])
    return jnp.concatenate(
        [plus(kept_a, pair(passed_a, x, 4, 3)), plus(kept_b, pair(passed_b, x, 4, 2))], axis=-1
    )


def on_device(
    hidden, final_states, logp_grad, value_weight, returns, advantages, log_ratio, lengths
):
    rows, depth = logp_grad.shape
    half = depth // 2
    width = half // CHUNKS
    units = hidden.shape[1]
    xl, y, c, z, xh = (lax.axis_index(a) for a in AXES)

    grad = logp_grad.reshape(rows, 2, half)
    mine, theirs = pick(grad, c, 1), pick(grad, 1 - c, 1)
    swapped = flip(theirs, "c")
    gathered = []
    for i in range(CHUNKS):
        cols = slice(i * width, (i + 1) * width)
        block = jnp.stack([mine[:, cols], swapped[:, cols]])
        gathered.append(lax.all_gather(block, "z"))

    blocks = hidden.reshape(8, 2, rows, units)
    kept, sent = pick(blocks, xh, 1), pick(blocks, 1 - xh, 1)
    across = flip(sent, "xh")
    kept_c, across_c = flip(kept, "c"), flip(across, "c")
    left = jnp.concatenate(
        [
            jnp.stack([kept, kept_c], axis=1).reshape(16 * rows, units).T,
            jnp.stack([across, across_c], axis=1).reshape(16 * rows, units).T,
        ]
    )

    policy_scale, value_scale = token_scales(
        final_states, value_weight, returns, advantages, log_ratio, lengths
    )
    head = lax.dynamic_slice_in_dim(value_weight.astype(jnp.float32), c * half, half)

    done = []
    for i in range(CHUNKS):
        cols = slice(i * width, (i + 1) * width)
        grad_rows = (
            policy_scale[..., None] * gathered[i].astype(jnp.float32)
            + value_scale[..., None] * head[cols]
        ).astype(jnp.bfloat16)
        term = jnp.dot(
            left, grad_rows.reshape(16 * rows, width), preferred_element_type=jnp.float32
        ).astype(jnp.bfloat16)
        term = term.reshape(2, 2, 4, units // 8, width)
        quarter = jnp.stack([scatter_y(term[0], y, 1), scatter_y(term[1], y, 3)])
        done.append(scatter_x(quarter, xl))
    whole = jnp.concatenate(done, axis=-1).reshape(2, units // 16, half)
    near, far = pick(whole, c, 0), flip(pick(whole, 1 - c, 0), "c")
    return jnp.where(
        c == 0, jnp.concatenate([near, far], axis=1), jnp.concatenate([far, near], axis=1)
    )


def solution(mesh):
    fine = Mesh(mesh.devices.reshape(2, 4, 2, 8, 2), AXES)
    dp, tensor = ("xl", "y", "c"), ("z", "xh")
    placed = (
        P(dp, tensor),
        P(dp + tensor, None),
        P(dp + tensor, None),
        P(),
        P(dp + tensor),
        P(dp + tensor),
        P(dp + tensor),
        P(),
    )
    return jax.shard_map(
        on_device, mesh=fine, in_specs=placed, out_specs=P(tensor + dp, None), check_vma=False
    )
```

```python
import jax
import jax.numpy as jnp
from jax import lax
from jax.sharding import Mesh, PartitionSpec as P

AXES = ("xl", "y", "c", "z", "xh")
GATHERS = (((10, "x"),), ((6, "y"),))
LANES = 128
X = ("xl", "xh")


def flip(v, axis):
    return lax.ppermute(v, axis, [(0, 1), (1, 0)])


def shift(v, axis, n, by):
    return lax.ppermute(v, axis, [(i, (i + by) % n) for i in range(n)])


def pair(v, axis, n, mask):
    return lax.ppermute(v, axis, [(i, i ^ mask) for i in range(n)])


def pick(v, index, axis):
    return lax.dynamic_index_in_dim(v, index, axis, keepdims=False)


def plus(a, b):
    return (a.astype(jnp.float32) + b.astype(jnp.float32)).astype(jnp.bfloat16)


def after(v, *earlier):
    return lax.optimization_barrier((v,) + earlier)[0]


def split(v):
    high = lax.reduce_precision(v, 8, 7)
    middle = lax.reduce_precision(v - high, 8, 7)
    return [high, middle, v - high - middle]


def merge(one, two):
    n = one[0:1] + two[0:1]
    off = one[1:2] / jnp.maximum(one[0:1], 1.0) - two[1:2] / jnp.maximum(two[0:1], 1.0)
    apart = off * off * (one[0:1] * two[0:1] / jnp.maximum(n, 1.0))
    row = lax.broadcasted_iota(jnp.int32, one.shape, 0)
    return one + two + jnp.where(row == 2, apart, 0.0)


def moments(advantages, live, before_x):
    part = jnp.stack([live, live * advantages] + [jnp.zeros_like(live)] * 6)
    for axis, n, mask in (("y", 4, 1), ("y", 4, 3), ("c", 2, 1), ("z", 8, 1), ("z", 8, 2), ("z", 8, 4)):
        part = merge(part, pair(part, axis, n, mask))
    part = after(part, before_x)
    for mask in (2, 3):
        part = merge(part, pair(part, X, 4, mask))
    count = jnp.sum(part[0])
    average = jnp.sum(part[1]) / count
    off = part[1] / jnp.maximum(part[0], 1.0) - average
    return average, jnp.sum(part[2] + part[0] * off * off) / count


def exchange(one, two, take, axis, masks):
    first, second = masks
    both = first ^ second
    got_one = pair(jnp.stack([take(one, first), take(one, both)]), axis, 4, first)
    got_two = pair(jnp.stack([take(two, second), take(two, both)]), axis, 4, second)
    passed_one = plus(take(one, second), got_one[1])
    passed_two = plus(take(two, first), got_two[1])
    kept_one = plus(take(one, 0), got_one[0])
    kept_two = plus(take(two, 0), got_two[0])
    return (
        plus(kept_one, pair(passed_one, axis, 4, second)),
        plus(kept_two, pair(passed_two, axis, 4, first)),
        (got_one, got_two),
    )


def on_device(
    hidden, final_states, logp_grad, value_weight, returns, advantages, log_ratio, lengths
):
    rows, depth = logp_grad.shape
    half = depth // 2
    units = hidden.shape[1]
    xl, y, c, z, xh = (lax.axis_index(a) for a in AXES)
    widths = [half // 16 * sum(n for n, _ in pieces) for pieces in GATHERS]
    starts = [sum(widths[:i]) for i in range(len(widths))]

    mine, theirs = [
        lax.dynamic_slice_in_dim(logp_grad, k * half, half, 1) for k in (c, 1 - c)
    ]
    swapped = flip(theirs, "c")

    group = (xl * 4 + y) * 2 + c
    place = (2 * z + xh) * rows + jnp.arange(rows, dtype=jnp.int32)
    live_here = (place < lengths[group]).astype(jnp.float32)
    values = jnp.dot(final_states, value_weight, preferred_element_type=jnp.float32)
    columns = advantages, log_ratio, 0.5 * live_here * (values - returns)
    own = jnp.concatenate([part for v in columns for part in split(v[:, None])], axis=1)
    own = jnp.pad(own, ((0, 0), (0, LANES - 9))).astype(jnp.bfloat16)
    scalars = jnp.concatenate([own, flip(own, "c")])

    gathered = []
    for i, (w, at) in enumerate(zip(widths, starts)):
        block = jnp.concatenate([mine[:, at : at + w], swapped[:, at : at + w]])
        if i == 0:
            block = jnp.concatenate([scalars, block], axis=1)
        else:
            block = after(block, gate)
        gate = block
        gathered.append(lax.all_gather(block, "z", tiled=True))

    blocks = hidden.reshape(8, 2, rows, units)
    kept, sent = pick(blocks, xh, 1), pick(blocks, 1 - xh, 1)
    across = flip(sent, "xh")
    average, spread = moments(advantages, live_here, across)
    left = [
        jnp.concatenate([v, flip(v, "c")], axis=1).reshape(-1, units) for v in (kept, across)
    ]
    gathered[0] = after(gathered[0], average, spread, *left)

    column = gathered[0][:, :LANES].astype(jnp.float32)
    gathered[0] = gathered[0][:, LANES:]
    adv, ratio, value_scale = [jnp.sum(column[:, k : k + 3], 1, keepdims=True) for k in (0, 3, 6)]
    token = lax.broadcasted_iota(jnp.int32, (16 * rows, 1), 0)
    places = (2 * (token // (2 * rows)) + xh) * rows + token % rows
    limits = jnp.where(token // rows % 2 == 0, lengths[group], lengths[group ^ 1])
    live = (places < limits).astype(jnp.float32)
    whitened = (adv - average) * lax.rsqrt(spread + 1e-05)
    clipped = (whitened > 0) & (ratio > jnp.log(1.2)) | (whitened < 0) & (ratio < jnp.log(0.8))
    active = jnp.where(clipped, 0.0, 1.0).astype(jnp.float32)
    policy_scale = -live * jnp.exp(ratio) * whitened * active
    head = lax.dynamic_slice_in_dim(value_weight.astype(jnp.float32), c * half, half)

    def take_x(v, m):
        return pick(v[m & 1], xl ^ (m >> 1), 0)

    def take_y0(v, m):
        return pick(v, y ^ m, 0)

    def take_y1(v, m):
        return pick(v, y ^ m, 1)

    near, far, first = [], [], ()
    for pieces, whole, start in zip(GATHERS, gathered, starts):
        whole = after(whole, *first)
        at, first = 0, ()
        for sixteenths, order in pieces:
            w = half // 16 * sixteenths

            def products(low, high):
                cut = slice(start + at + low, start + at + high)
                grad_rows = (
                    policy_scale * whole[:, at + low : at + high].astype(jnp.float32)
                    + value_scale * head[cut]
                ).astype(jnp.bfloat16)
                grad_rows = lax.optimization_barrier(grad_rows)
                return [
                    lax.dot_general(
                        v, grad_rows, (((0,), (0,)), ((), ())), preferred_element_type=jnp.float32
                    ).astype(jnp.bfloat16).reshape(2, 4, units // 8, high - low)
                    for v in left
                ]

            if order == "x":
                a, b = products(0, w // 2), products(w // 2, w)
                a, b, got = exchange(a, b, take_x, X, (2, 3))
                a, b, _ = exchange(a, b, take_y0, "y", (1, 3))
            else:
                *both, got = exchange(*products(0, w), take_y1, "y", (1, 3))
                cuts = slice(w // 2), slice(w // 2, w)
                a, b = [[t[..., cut] for t in both] for cut in cuts]
                a, b, _ = exchange(a, b, take_x, X, (2, 3))
            at += w
            first += got
            done = jnp.concatenate([a, b], axis=1).reshape(2, units // 16, w)
            near.append(pick(done, c, 0))
            far.append(flip(pick(done, 1 - c, 0), "c"))
    near, far = jnp.concatenate(near, axis=1), jnp.concatenate(far, axis=1)
    return jnp.where(
        c == 0, jnp.concatenate([near, far], axis=1), jnp.concatenate([far, near], axis=1)
    )


def solution(mesh):
    fine = Mesh(mesh.devices.reshape(2, 4, 2, 8, 2), AXES)
    dp, tensor = ("xl", "y", "c"), ("z", "xh")
    placed = (
        P(dp, tensor),
        P(dp + tensor, None),
        P(dp + tensor, None),
        P(),
        P(dp + tensor),
        P(dp + tensor),
        P(dp + tensor),
        P(),
    )
    return jax.shard_map(
        on_device, mesh=fine, in_specs=placed, out_specs=P(tensor + dp, None), check_vma=False
    )
```

```python
import jax
import jax.numpy as jnp
from jax import lax
from jax.sharding import Mesh, PartitionSpec as P

AXES = ("xl", "y", "c", "z", "xh")
GATHERS = (((12, "x"),), ((4, "y"),))
LANES = 128
X = ("xl", "xh")


def flip(v, axis):
    return lax.ppermute(v, axis, [(0, 1), (1, 0)])


def shift(v, axis, n, by):
    return lax.ppermute(v, axis, [(i, (i + by) % n) for i in range(n)])


def pair(v, axis, n, mask):
    return lax.ppermute(v, axis, [(i, i ^ mask) for i in range(n)])


def pick(v, index, axis):
    return lax.dynamic_index_in_dim(v, index, axis, keepdims=False)


def plus(a, b):
    return (a.astype(jnp.float32) + b.astype(jnp.float32)).astype(jnp.bfloat16)


def after(v, *earlier):
    return lax.optimization_barrier((v,) + earlier)[0]


def split(v):
    high = lax.reduce_precision(v, 8, 7)
    middle = lax.reduce_precision(v - high, 8, 7)
    return [high, middle, v - high - middle]


def merge(one, two):
    n = one[0:1] + two[0:1]
    off = one[1:2] / jnp.maximum(one[0:1], 1.0) - two[1:2] / jnp.maximum(two[0:1], 1.0)
    apart = off * off * (one[0:1] * two[0:1] / jnp.maximum(n, 1.0))
    row = lax.broadcasted_iota(jnp.int32, one.shape, 0)
    return one + two + jnp.where(row == 2, apart, 0.0)


def moments(advantages, live, before_x):
    part = jnp.stack([live, live * advantages] + [jnp.zeros_like(live)] * 6)
    for axis, n, mask in (("y", 4, 1), ("y", 4, 3), ("c", 2, 1), ("z", 8, 1), ("z", 8, 2), ("z", 8, 4)):
        part = merge(part, pair(part, axis, n, mask))
    part = after(part, before_x)
    for mask in (2, 3):
        part = merge(part, pair(part, X, 4, mask))
    count = jnp.sum(part[0])
    average = jnp.sum(part[1]) / count
    off = part[1] / jnp.maximum(part[0], 1.0) - average
    return average, jnp.sum(part[2] + part[0] * off * off) / count


def exchange(one, two, take, axis, masks):
    first, second = masks
    both = first ^ second
    got_one = pair(jnp.stack([take(one, first), take(one, both)]), axis, 4, first)
    got_two = pair(jnp.stack([take(two, second), take(two, both)]), axis, 4, second)
    passed_one = plus(take(one, second), got_one[1])
    passed_two = plus(take(two, first), got_two[1])
    kept_one = plus(take(one, 0), got_one[0])
    kept_two = plus(take(two, 0), got_two[0])
    return (
        plus(kept_one, pair(passed_one, axis, 4, second)),
        plus(kept_two, pair(passed_two, axis, 4, first)),
        (got_one, got_two),
    )


def direct(share, axis):
    got = [pair(share(m), axis, 4, m) for m in (1, 2, 3)]
    return sum((v.astype(jnp.float32) for v in got), share(0).astype(jnp.float32)).astype(jnp.bfloat16)


def on_device(
    hidden, final_states, logp_grad, value_weight, returns, advantages, log_ratio, lengths
):
    rows, depth = logp_grad.shape
    half = depth // 2
    units = hidden.shape[1]
    xl, y, c, z, xh = (lax.axis_index(a) for a in AXES)
    widths = [half // 16 * sum(n for n, _ in pieces) for pieces in GATHERS]
    starts = [sum(widths[:i]) for i in range(len(widths))]

    mine, theirs = [
        lax.dynamic_slice_in_dim(logp_grad, k * half, half, 1) for k in (c, 1 - c)
    ]
    swapped = flip(theirs, "c")

    group = (xl * 4 + y) * 2 + c
    place = (2 * z + xh) * rows + jnp.arange(rows, dtype=jnp.int32)
    live_here = (place < lengths[group]).astype(jnp.float32)
    values = jnp.dot(final_states, value_weight, preferred_element_type=jnp.float32)
    columns = advantages, log_ratio, 0.5 * live_here * (values - returns)
    own = jnp.concatenate([part for v in columns for part in split(v[:, None])], axis=1)
    own = jnp.pad(own, ((0, 0), (0, LANES - 9))).astype(jnp.bfloat16)
    scalars = jnp.concatenate([own, flip(own, "c")])

    gathered = []
    for i, (w, at) in enumerate(zip(widths, starts)):
        block = jnp.concatenate([mine[:, at : at + w], swapped[:, at : at + w]])
        if i == 0:
            block = jnp.concatenate([scalars, block], axis=1)
        else:
            block = after(block, gate)
        gate = block
        gathered.append(lax.all_gather(block, "z", tiled=True))

    blocks = hidden.reshape(8, 2, rows, units)
    kept, sent = pick(blocks, xh, 1), pick(blocks, 1 - xh, 1)
    across = flip(sent, "xh")
    average, spread = moments(advantages, live_here, across)
    left = [
        jnp.concatenate([v, flip(v, "c")], axis=1).reshape(-1, units) for v in (kept, across)
    ]
    gathered[0] = after(gathered[0], average, spread, *left)

    column = gathered[0][:, :LANES].astype(jnp.float32)
    gathered[0] = gathered[0][:, LANES:]
    adv, ratio, value_scale = [jnp.sum(column[:, k : k + 3], 1, keepdims=True) for k in (0, 3, 6)]
    token = lax.broadcasted_iota(jnp.int32, (16 * rows, 1), 0)
    places = (2 * (token // (2 * rows)) + xh) * rows + token % rows
    limits = jnp.where(token // rows % 2 == 0, lengths[group], lengths[group ^ 1])
    live = (places < limits).astype(jnp.float32)
    whitened = (adv - average) * lax.rsqrt(spread + 1e-05)
    clipped = (whitened > 0) & (ratio > jnp.log(1.2)) | (whitened < 0) & (ratio < jnp.log(0.8))
    active = jnp.where(clipped, 0.0, 1.0).astype(jnp.float32)
    policy_scale = -live * jnp.exp(ratio) * whitened * active
    head = lax.dynamic_slice_in_dim(value_weight.astype(jnp.float32), c * half, half)

    def take_x(v, m):
        return pick(v[m & 1], xl ^ (m >> 1), 0)

    def take_y0(v, m):
        return pick(v, y ^ m, 0)

    def take_y1(v, m):
        return pick(v, y ^ m, 1)

    near, far, first = [], [], ()
    for pieces, whole, start in zip(GATHERS, gathered, starts):
        at = 0
        for sixteenths, order in pieces:
            w = half // 16 * sixteenths

            def products(low, high):
                cut = slice(start + at + low, start + at + high)
                grad_rows = (
                    policy_scale * whole[:, at + low : at + high].astype(jnp.float32)
                    + value_scale * head[cut]
                ).astype(jnp.bfloat16)
                grad_rows = lax.optimization_barrier(grad_rows)
                return [
                    lax.dot_general(
                        v, grad_rows, (((0,), (0,)), ((), ())), preferred_element_type=jnp.float32
                    ).astype(jnp.bfloat16).reshape(2, 4, units // 8, high - low)
                    for v in left
                ]

            if order == "x":
                a, b = products(0, w // 2), products(w // 2, w)
                *both, got = exchange(a, b, take_x, X, (2, 3))
                done = direct(
                    lambda m: jnp.concatenate([take_y0(v, m) for v in both], axis=1), "y"
                )
            else:
                terms = [after(v, *first) for v in products(0, w)]
                *both, got = exchange(*terms, take_y1, "y", (1, 3))
                done = direct(lambda m: take_x(both, m), X)
            at += w
            first = got
            done = done.reshape(2, units // 16, w)
            near.append(pick(done, c, 0))
            far.append(flip(pick(done, 1 - c, 0), "c"))
    near, far = jnp.concatenate(near, axis=1), jnp.concatenate(far, axis=1)
    return jnp.where(
        c == 0, jnp.concatenate([near, far], axis=1), jnp.concatenate([far, near], axis=1)
    )


def solution(mesh):
    fine = Mesh(mesh.devices.reshape(2, 4, 2, 8, 2), AXES)
    dp, tensor = ("xl", "y", "c"), ("z", "xh")
    placed = (
        P(dp, tensor),
        P(dp + tensor, None),
        P(dp + tensor, None),
        P(),
        P(dp + tensor),
        P(dp + tensor),
        P(dp + tensor),
        P(),
    )
    return jax.shard_map(
        on_device, mesh=fine, in_specs=placed, out_specs=P(tensor + dp, None), check_vma=False
    )
```

```python
import jax
import jax.numpy as jnp
from jax import lax
from jax.sharding import Mesh, PartitionSpec as P

AXES = ("xl", "y", "c", "z", "xh")
GATHERS = (((12, "x"),), ((4, "y"),))
LANES = 128
X = ("xl", "xh")


def flip(v, axis):
    return lax.ppermute(v, axis, [(0, 1), (1, 0)])


def shift(v, axis, n, by):
    return lax.ppermute(v, axis, [(i, (i + by) % n) for i in range(n)])


def pair(v, axis, n, mask):
    return lax.ppermute(v, axis, [(i, i ^ mask) for i in range(n)])


def pick(v, index, axis):
    return lax.dynamic_index_in_dim(v, index, axis, keepdims=False)


def plus(a, b):
    return (a.astype(jnp.float32) + b.astype(jnp.float32)).astype(jnp.bfloat16)


def after(v, *earlier):
    return lax.optimization_barrier((v,) + earlier)[0]


def split(v):
    high = lax.reduce_precision(v, 8, 7)
    middle = lax.reduce_precision(v - high, 8, 7)
    return [high, middle, v - high - middle]


def merge(one, two):
    n = one[0:1] + two[0:1]
    off = one[1:2] / jnp.maximum(one[0:1], 1.0) - two[1:2] / jnp.maximum(two[0:1], 1.0)
    apart = off * off * (one[0:1] * two[0:1] / jnp.maximum(n, 1.0))
    row = lax.broadcasted_iota(jnp.int32, one.shape, 0)
    return one + two + jnp.where(row == 2, apart, 0.0)


def moments(advantages, live, before_x):
    part = jnp.stack([live, live * advantages] + [jnp.zeros_like(live)] * 6)
    for axis, n, mask in (("y", 4, 1), ("y", 4, 3), ("c", 2, 1), ("z", 8, 1), ("z", 8, 2), ("z", 8, 4)):
        part = merge(part, pair(part, axis, n, mask))
    part = after(part, before_x)
    for mask in (2, 3):
        part = merge(part, pair(part, X, 4, mask))
    count = jnp.sum(part[0])
    average = jnp.sum(part[1]) / count
    off = part[1] / jnp.maximum(part[0], 1.0) - average
    return average, jnp.sum(part[2] + part[0] * off * off) / count


def exchange(one, two, take, axis, masks):
    first, second = masks
    both = first ^ second
    got_one = pair(jnp.stack([take(one, first), take(one, both)]), axis, 4, first)
    got_two = pair(jnp.stack([take(two, second), take(two, both)]), axis, 4, second)
    passed_one = plus(take(one, second), got_one[1])
    passed_two = plus(take(two, first), got_two[1])
    kept_one = plus(take(one, 0), got_one[0])
    kept_two = plus(take(two, 0), got_two[0])
    return (
        plus(kept_one, pair(passed_one, axis, 4, second)),
        plus(kept_two, pair(passed_two, axis, 4, first)),
        (got_one, got_two),
    )


def direct(share, axis):
    got = [pair(share(m), axis, 4, m) for m in (1, 2, 3)]
    return sum((v.astype(jnp.float32) for v in got), share(0).astype(jnp.float32)).astype(jnp.bfloat16)


def on_device(
    hidden, final_states, logp_grad, value_weight, returns, advantages, log_ratio, lengths
):
    rows, depth = logp_grad.shape
    half = depth // 2
    units = hidden.shape[1]
    xl, y, c, z, xh = (lax.axis_index(a) for a in AXES)
    widths = [half // 16 * sum(n for n, _ in pieces) for pieces in GATHERS]
    starts = [sum(widths[:i]) for i in range(len(widths))]

    mine, theirs = [
        lax.dynamic_slice_in_dim(logp_grad, k * half, half, 1) for k in (c, 1 - c)
    ]
    swapped = flip(theirs, "c")

    group = (xl * 4 + y) * 2 + c
    place = (2 * z + xh) * rows + jnp.arange(rows, dtype=jnp.int32)
    live_here = (place < lengths[group]).astype(jnp.float32)
    values = jnp.dot(final_states, value_weight, preferred_element_type=jnp.float32)
    columns = advantages, log_ratio, 0.5 * live_here * (values - returns)
    own = jnp.concatenate([part for v in columns for part in split(v[:, None])], axis=1)
    own = jnp.pad(own, ((0, 0), (0, LANES - 9))).astype(jnp.bfloat16)
    scalars = jnp.concatenate([own, flip(own, "c")])

    gathered = []
    for i, (w, at) in enumerate(zip(widths, starts)):
        block = jnp.concatenate([mine[:, at : at + w], swapped[:, at : at + w]])
        if i == 0:
            block = jnp.concatenate([scalars, block], axis=1)
        else:
            block = after(block, gate)
        gate = block
        gathered.append(lax.all_gather(block, "z", tiled=True))

    blocks = hidden.reshape(8, 2, rows, units)
    kept, sent = pick(blocks, xh, 1), pick(blocks, 1 - xh, 1)
    across = flip(sent, "xh")
    average, spread = moments(advantages, live_here, across)
    left = [
        jnp.concatenate([v, flip(v, "c")], axis=1).reshape(-1, units) for v in (kept, across)
    ]
    gathered[0] = after(gathered[0], average, spread, *left)

    column = gathered[0][:, :LANES].astype(jnp.float32)
    gathered[0] = gathered[0][:, LANES:]
    adv, ratio, value_scale = [jnp.sum(column[:, k : k + 3], 1, keepdims=True) for k in (0, 3, 6)]
    token = lax.broadcasted_iota(jnp.int32, (16 * rows, 1), 0)
    places = (2 * (token // (2 * rows)) + xh) * rows + token % rows
    limits = jnp.where(token // rows % 2 == 0, lengths[group], lengths[group ^ 1])
    live = (places < limits).astype(jnp.float32)
    whitened = (adv - average) * lax.rsqrt(spread + 1e-05)
    clipped = (whitened > 0) & (ratio > jnp.log(1.2)) | (whitened < 0) & (ratio < jnp.log(0.8))
    active = jnp.where(clipped, 0.0, 1.0).astype(jnp.float32)
    policy_scale = -live * jnp.exp(ratio) * whitened * active
    head = lax.dynamic_slice_in_dim(value_weight.astype(jnp.float32), c * half, half)

    def take_x(v, m):
        return pick(v[m & 1], xl ^ (m >> 1), 0)

    def take_y0(v, m):
        return pick(v, y ^ m, 0)

    def take_y1(v, m):
        return pick(v, y ^ m, 1)

    near, far, first = [], [], ()
    for pieces, whole, start in zip(GATHERS, gathered, starts):
        at = 0
        for sixteenths, order in pieces:
            w = half // 16 * sixteenths

            def products(low, high):
                cut = slice(start + at + low, start + at + high)
                grad_rows = (
                    policy_scale * whole[:, at + low : at + high].astype(jnp.float32)
                    + value_scale * head[cut]
                ).astype(jnp.bfloat16)
                grad_rows = lax.optimization_barrier(grad_rows)
                return [
                    lax.dot_general(
                        v, grad_rows, (((0,), (0,)), ((), ())), preferred_element_type=jnp.float32
                    ).astype(jnp.bfloat16).reshape(2, 4, units // 8, high - low)
                    for v in left
                ]

            if order == "x":
                a, b = products(0, w // 2), products(w // 2, w)
                *both, got = exchange(a, b, take_x, X, (2, 3))
                a, b, _ = exchange(*both, take_y0, "y", (1, 3))
                done = jnp.concatenate([a, b], axis=1)
            else:
                terms = [after(v, *first) for v in products(0, w)]
                *both, got = exchange(*terms, take_y1, "y", (1, 3))
                done = direct(lambda m: take_x(both, m), X)
            at += w
            first = got
            done = done.reshape(2, units // 16, w)
            near.append(pick(done, c, 0))
            far.append(flip(pick(done, 1 - c, 0), "c"))
    near, far = jnp.concatenate(near, axis=1), jnp.concatenate(far, axis=1)
    return jnp.where(
        c == 0, jnp.concatenate([near, far], axis=1), jnp.concatenate([far, near], axis=1)
    )


def solution(mesh):
    fine = Mesh(mesh.devices.reshape(2, 4, 2, 8, 2), AXES)
    dp, tensor = ("xl", "y", "c"), ("z", "xh")
    placed = (
        P(dp, tensor),
        P(dp + tensor, None),
        P(dp + tensor, None),
        P(),
        P(dp + tensor),
        P(dp + tensor),
        P(dp + tensor),
        P(),
    )
    return jax.shard_map(
        on_device, mesh=fine, in_specs=placed, out_specs=P(tensor + dp, None), check_vma=False
    )
```
